512 devices in a mesh: rep: 32 (over x, z), exp: 16 (over y, core).
Axes of the slice: x: 4, y: 8, z: 8, core: 2. Of those that a mesh axis runs over, the one named last changes fastest.
Arguments:
- tokens: bfloat16 [65536, 2048], P(('rep', 'exp')), may hold values from -6 to 6
- expert_ids: int32 [65536, 1], P(('rep', 'exp')), may hold values from 0 to 3; in each aligned block of 128 rows (0 to 127, 128 to 255, ...) at most 32 rows name the same one
- gate_prob: float32 [65536], P(('rep', 'exp')), may hold values from 0.05 to 1
- cotangent: bfloat16 [65536, 2048], P(('rep', 'exp')), may hold values from -6 to 6
- w_gate: bfloat16 [32, 2048, 4096], P('rep', None, 'exp'), may hold values from -0.125 to 0.125
- w_up: bfloat16 [32, 2048, 4096], P('rep', None, 'exp'), may hold values from -0.125 to 0.125
- w_down: bfloat16 [32, 4096, 2048], P('rep', 'exp'), may hold values from -0.1875 to 0.1875
- touched: int32 [32, 256], P('rep', 'exp'), may hold values 0 or 1
Outputs:
- mixed: bfloat16 [65536, 2048], P(('rep', 'exp'))
- averaged: bfloat16 [4096, 6144], P('exp', 'rep')
The draws below stay inside these ranges and needn't reach their ends.
Inputs may be any that keep to these rules, and one draw needn't show every extreme that they name: `expert_ids`: the rows of one device name each of the 4 window experts exactly 32 times.
All inputs are finite; a program needn't handle non-finite values. No bound on the sum of `touched` on one device may be relied on, other than what follows from the above.
Results may differ from the reference program's by a relative error of at most 0.018.
Values may be sent and summed in bfloat16 or wider, within the bound.
No kernel may reach another device: no remote copies, remote signals or barrier semaphores. Data moves between devices by JAX's collectives and lax.ppermute only.
A program may use at most 64 MiB of HBM per device.

```python
import math
import jax
import jax.numpy as jnp
import numpy as np
from jax import lax

D = 2048
FF = 1024
EW = 4
TILE = 16
ROWS_DEV = 128
CAP = 32
SHARDS = 4
HID = 256
NTILE = 256
REPS = 32
TOKENS = 65536
N_EXP = 16


def plant(drawn, rng, smallest, largest):
    spot = [jax.random.randint(jax.random.fold_in(rng, axis), (), 0, length) for axis, length in enumerate(drawn.shape)]
    longest = drawn.shape.index(max(drawn.shape))
    neighbour = spot[:longest] + [(spot[longest] + 1) % drawn.shape[longest]] + spot[longest + 1:]
    return drawn.at[tuple(spot)].set(smallest).at[tuple(neighbour)].set(largest)


def block_levels(own_key, shape, cuts, low, top_value):
    def one(dim, blocks):
        draws = jax.random.uniform(jax.random.fold_in(jax.random.fold_in(own_key, 6), dim), (blocks,), jnp.float32, low / len(cuts), top_value / len(cuts))
        return jnp.repeat(jnp.exp(draws), shape[dim] // blocks).reshape((-1,) + (1,) * (len(shape) - dim - 1))

    gain = one(*cuts[0])
    for cut in cuts[1:]:
        gain = gain * one(*cut)
    return gain


def routed_block(stream_key, own, number, rows, count, top, limit, lean):
    sequence = jax.random.permutation(stream_key, count)
    heavy_load, usual = portions_of(count, rows * top, limit, lean, True), portions_of(count, rows * top, limit, lean, False)
    places = jnp.arange(count)

    def named(sizes, offset_by):
        used = int((sizes > 0).sum())
        fixed = max(1, used // 4)
        moved = fixed + (places - fixed + offset_by * (used - fixed)) % max(1, count - fixed)
        return jnp.zeros((count,), jnp.int32).at[sequence[jnp.where(places < fixed, places, moved)]].set(jnp.asarray(sizes, jnp.int32))

    sizes = jnp.where(number % 4 == 0, named(heavy_load, number // 4), named(usual, number - number // 4 - 1))
    mixed = jax.random.permutation(jax.random.fold_in(own, 3), count)
    donor, sink = mixed[0:count // 2 * 2:2], mixed[1:count // 2 * 2:2]
    room = jnp.minimum(sizes[donor] - 1, limit - sizes[sink]) // 2
    room = jnp.where((donor == sequence[0]) | (sink == sequence[0]) | (sizes[sink] == 0), 0, jnp.maximum(room, 0))
    moved = jax.random.randint(jax.random.fold_in(own, 4), (count // 2,), 0, 1 << 20) % (room + 1)
    sizes = sizes.at[donor].add(-moved).at[sink].add(moved)
    labels = jnp.searchsorted(jnp.cumsum(sizes), jnp.arange(rows * top), side="right").astype(jnp.int32)
    table = labels.reshape(top, rows).T
    table = table[jax.random.permutation(jax.random.fold_in(own, 1), rows)]
    offset_by = jax.random.randint(jax.random.fold_in(own, 2), (rows, 1), 0, top)
    return jnp.take_along_axis(table, (jnp.arange(top)[None, :] + offset_by) % top, axis=1)


def portions_of(count, total, most, lean, full):
    portions = [(1 << 20) // math.isqrt(standing ** lean) + 1 for standing in range(1, count + 1)]
    largest = most if full else min(most, max(-(-total // count), total * portions[0] // sum(portions)))
    least = 1 if total - largest >= count - 1 else 0
    given, surplus = [largest] + [least] * (count - 1), total - largest - least * (count - 1)
    while surplus > 0:
        candidates = [i for i in range(1, count) if given[i] < largest] or [i for i in range(1, count) if given[i] < most]
        pool, remaining = sum([portions[i] for i in candidates]), surplus
        for i in candidates:
            more = min(most - given[i], max(1, remaining * portions[i] // pool), surplus)
            given[i] = given[i] + more
            surplus = surplus - more
    return np.array(given)


def bell_draw(stream_key, shape, scale, most, cuts=(), held_as=jnp.bfloat16):
    values = jax.random.normal(stream_key, shape, jnp.float32) * scale
    if len(cuts) > 0:
        values = block_levels(stream_key, shape, cuts, -0.22, 0.18) * values
    return jnp.clip(values, min=-most, max=most).astype(held_as)


def setup_inputs(seed: int = 0) -> dict:
    streams_of = jax.random.split(jax.random.key(seed), 9)
    tokens = bell_draw(streams_of[0], (TOKENS, D), 1.0, 6.0, ((0, 512),))
    expert_ids_keys = jax.random.split(jax.random.fold_in(streams_of[1], 1), TOKENS // ROWS_DEV)
    expert_ids_turns = jax.random.permutation(jax.random.fold_in(streams_of[1], 3), TOKENS // ROWS_DEV)
    expert_ids = jax.vmap(lambda own, number: routed_block(jax.random.fold_in(streams_of[1], 2), own, number, ROWS_DEV, EW, 1, CAP, 0))(expert_ids_keys, expert_ids_turns).reshape((TOKENS, 1))
    gate_prob = jnp.clip(jnp.exp(math.log(1.0) - 2.9957323 * jax.random.uniform(streams_of[2], (TOKENS,), jnp.float32) ** block_levels(streams_of[2], (TOKENS,), ((0, 512),), -0.2, 0.2)), 0.05, 1.0)
    cotangent = bell_draw(streams_of[3], (TOKENS, D), 1.0, 6.0, ((0, 512),))
    w_gate = bell_draw(streams_of[4], (REPS, D, EW * FF), D ** -0.5, 0.125, ((0, 32), (2, 16)))
    w_up = bell_draw(streams_of[5], (REPS, D, EW * FF), D ** -0.5, 0.125, ((0, 32), (2, 16)))
    w_down = bell_draw(streams_of[6], (REPS, EW * FF, D), FF ** -0.5, 0.1875, ((0, 32), (1, 16)))
    touched = plant((jax.random.randint(streams_of[7], (REPS, NTILE), 0, 2) < 1).astype(jnp.int32), jax.random.fold_in(streams_of[7], 1), 0, 1)
    return {"tokens": tokens, "expert_ids": expert_ids, "gate_prob": gate_prob, "cotangent": cotangent, "w_gate": w_gate, "w_up": w_up, "w_down": w_down, "touched": touched}


def swish_slope(h):
    s = jax.nn.sigmoid(h)
    return s * (1.0 + h * (1.0 - s))


def one_replica(xrows, ids, gate, cot, wg, wu, wd, mask):
    dy = (gate[:, None] * cot.astype(jnp.float32)).astype(jnp.bfloat16)
    mixed = jnp.zeros(xrows.shape, jnp.float32)
    blocks = []
    for e in range(EW):
        rows_e = ids[:, 0] == e
        wg_e = wg[:, e * FF:(e + 1) * FF]
        wu_e = wu[:, e * FF:(e + 1) * FF]
        wd_e = wd[e * FF:(e + 1) * FF, :]
        h = jnp.dot(xrows, wg_e, preferred_element_type=jnp.float32)
        u = jnp.dot(xrows, wu_e, preferred_element_type=jnp.float32)
        act = (h * jax.nn.sigmoid(h) * u).astype(jnp.bfloat16)
        total = jnp.zeros(xrows.shape, jnp.float32)
        for s in range(SHARDS):
            part = jnp.dot(act[:, s * HID:(s + 1) * HID], wd_e[s * HID:(s + 1) * HID, :],
                           preferred_element_type=jnp.float32).astype(jnp.bfloat16)
            part = lax.optimization_barrier(part)
            total = total + part.astype(jnp.float32)
        mixed = jnp.where(rows_e[:, None], gate[:, None] * total, mixed)
        dy_e = jnp.where(rows_e[:, None], dy, jnp.zeros_like(dy))
        grad_a = jnp.dot(dy_e, wd_e.T, preferred_element_type=jnp.float32)
        d_down = jnp.dot(act.T, dy_e, preferred_element_type=jnp.float32)
        d_h = (grad_a * u * swish_slope(h)).astype(jnp.bfloat16)
        d_u = (grad_a * h * jax.nn.sigmoid(h)).astype(jnp.bfloat16)
        d_gate = jnp.dot(d_h.T, xrows, preferred_element_type=jnp.float32)
        d_upper = jnp.dot(d_u.T, xrows, preferred_element_type=jnp.float32)
        blocks.append(jnp.concatenate([d_gate, d_upper, d_down], axis=1))
    delta = jnp.concatenate(blocks, axis=0)
    scale = jnp.repeat(mask.astype(jnp.float32), TILE)
    rounded = lax.optimization_barrier((delta * scale[:, None]).astype(jnp.bfloat16))
    return mixed.astype(jnp.bfloat16), rounded


def reference(tokens, expert_ids, gate_prob, cotangent, w_gate, w_up, w_down, touched):
    per = N_EXP * ROWS_DEV
    xs = tokens.reshape(REPS, per, D)
    ids = expert_ids.reshape(REPS, per, 1)
    gates = gate_prob.reshape(REPS, per)
    cots = cotangent.reshape(REPS, per, D)

    def step(acc, items):
        xrows, idr, gate, cot, wg, wu, wd, mask = items
        mixed, delta = one_replica(xrows, idr, gate, cot, wg, wu, wd, mask)
        return acc + delta.astype(jnp.float32), mixed

    init = jnp.zeros((EW * FF, 3 * D), jnp.float32)
    acc, mixed = lax.scan(step, init, (xs, ids, gates, cots, w_gate, w_up, w_down, touched))
    averaged = (acc / REPS).astype(jnp.bfloat16)
    return mixed.reshape(TOKENS, D), averaged
```

```python
import jax
import jax.numpy as jnp
from jax import lax
from jax.sharding import Mesh, PartitionSpec as P

EW = 4
TILE = 16
X, Z, Y, C = 4, 8, 8, 2
AXES = ("x", "z", "y", "c")
bf16 = jnp.bfloat16
f32 = jnp.float32

PERM1 = [(i, (i - 1) % Y if i % 2 == 0 else (i + 1) % Y) for i in range(Y)]
PERM2 = [(i, (i + 2) % Y if i % 2 == 0 else (i - 2) % Y) for i in range(Y)]
PERM3 = [(i, ((i + 4) ^ 1) % Y) for i in range(Y)]
PAIR = [(i, i ^ 1) for i in range(Y)]
SWAP = [(0, 1), (1, 0)]


def swish_slope(h):
    s = jax.nn.sigmoid(h)
    return s * (1.0 + h * (1.0 - s))


def share(buf):
    parts = [
        buf[0],
        lax.ppermute(buf[1], "y", PERM1),
        lax.ppermute(buf[2], "y", PERM2),
        lax.ppermute(buf[3], "y", PERM3),
    ]
    mine = jnp.concatenate(parts, axis=0)
    both = jnp.concatenate([mine, lax.ppermute(mine, "y", PAIR)], axis=0)
    return jnp.concatenate([both, lax.ppermute(both, "c", SWAP)], axis=0)


def reduce_rep(part):
    n = part.shape[1]
    over_x = lax.all_to_all(part, "x", split_axis=0, concat_axis=0, tiled=True)
    sum_x = over_x.reshape(X, -1, n).astype(f32).sum(axis=0).astype(bf16)
    over_z = lax.all_to_all(sum_x, "z", split_axis=0, concat_axis=0, tiled=True)
    return over_z.reshape(Z, -1, n).astype(f32).sum(axis=0)


def body(tokens, expert_ids, gate_prob, cotangent, w_gate, w_up, w_down, touched):
    rows, width = tokens.shape
    cap = rows // EW
    y = lax.axis_index("y")
    odd = y % 2
    ids = expert_ids[:, 0]
    onehot = (expert_ids == jnp.arange(EW)[None, :]).astype(f32)
    lower = (
        lax.broadcasted_iota(jnp.int32, (rows, rows), 0)
        > lax.broadcasted_iota(jnp.int32, (rows, rows), 1)
    ).astype(f32)
    earlier = jnp.dot(lower, onehot)
    slot_of = jnp.sum(onehot * earlier, axis=1).astype(jnp.int32)
    away = (ids - y // 2) % EW
    place = jnp.where(away == 2, 3, jnp.where(away == 0, 0, jnp.where((away == 1) == (odd == 1), 1, 2)))
    target = place * cap + slot_of
    placer = (target[None, :] == jnp.arange(EW * cap)[:, None]).astype(bf16)
    dy = (gate_prob[:, None] * cotangent.astype(f32)).astype(bf16)
    x_buf = jnp.dot(placer, tokens, preferred_element_type=f32).astype(bf16).reshape(EW, cap, width)
    d_buf = jnp.dot(placer, dy, preferred_element_type=f32).astype(bf16).reshape(EW, cap, width)
    x_rows = share(x_buf)
    d_rows = share(d_buf)
    wg = w_gate[0]
    wu = w_up[0]
    wd = w_down[0]
    h = jnp.dot(x_rows, wg, preferred_element_type=f32)
    u = jnp.dot(x_rows, wu, preferred_element_type=f32)
    act = (h * jax.nn.sigmoid(h) * u).astype(bf16)
    partial_out = jnp.dot(act, wd, preferred_element_type=f32).astype(bf16)
    half = partial_out.shape[0] // 2
    core_sum = (
        partial_out[:half].astype(f32)
        + lax.ppermute(partial_out[half:], "c", SWAP).astype(f32)
    ).astype(bf16).reshape(Y, cap, width)

    grad_a = lax.dot_general(d_rows, wd, (((1,), (1,)), ((), ())), preferred_element_type=f32)
    mask = jnp.repeat(touched[0].astype(f32), TILE)[None, :]
    d_h = (grad_a * u * swish_slope(h) * mask).astype(bf16)
    d_u = (grad_a * h * jax.nn.sigmoid(h) * mask).astype(bf16)
    act_m = act * mask.astype(bf16)
    tdot = lambda a, b: lax.dot_general(a, b, (((0,), (0,)), ((), ())), preferred_element_type=f32).astype(bf16)
    delta = jnp.concatenate([tdot(x_rows, d_h), tdot(x_rows, d_u), tdot(d_rows, act_m)], axis=0)
    hid = delta.shape[1] // 2
    parts = [reduce_rep(delta[:, :hid]), reduce_rep(delta[:, hid:])]
    averaged = (jnp.concatenate(parts, axis=1) / (X * Z)).astype(bf16).T

    offset = (jnp.arange(Y) - y) % Y
    at_even = jnp.array([0, 4, 5, 6, 7, 3, 2, 1], jnp.int32)
    at_odd = jnp.array([0, 1, 2, 3, 7, 6, 5, 4], jnp.int32)
    order = jnp.where(odd == 1, at_odd, at_even)[offset]
    send = jnp.take(core_sum, order, axis=0, mode="clip")
    back = lax.all_to_all(send, "y", split_axis=0, concat_axis=0, tiled=True).reshape(Y * cap, width)
    column = jnp.arange(Y * cap)[None, :]
    picker = ((column // (2 * cap) == ids[:, None]) & (column % cap == slot_of[:, None])).astype(bf16)
    row_out = jnp.dot(picker, back, preferred_element_type=f32)
    mixed = (gate_prob[:, None] * row_out).astype(bf16)
    return mixed, averaged


def solution(mesh):
    fine = Mesh(mesh.devices.reshape(X, Z, Y, C), AXES)
    rep, exp = ("x", "z"), ("y", "c")
    return jax.shard_map(
        body,
        mesh=fine,
        in_specs=(
            P(AXES, None),
            P(AXES, None),
            P(AXES),
            P(AXES, None),
            P(rep, None, exp),
            P(rep, None, exp),
            P(rep, exp, None),
            P(rep, exp),
        ),
        out_specs=(P(AXES, None), P(exp, rep)),
        check_vma=False,
    )
```

```python
import functools

import jax
import jax.numpy as jnp
from jax import lax
from jax.experimental import pallas as pl
from jax.experimental.pallas import tpu as pltpu
from jax.sharding import Mesh, PartitionSpec as P

EW = 4
TILE = 16
X, Z, Y, C = 4, 8, 8, 2
AXES = ("x", "z", "y", "c")
CAP = 32
D = 2048
HID = 256
PART = 64
bf16 = jnp.bfloat16
f32 = jnp.float32

PERM1 = [(i, (i - 1) % Y if i % 2 == 0 else (i + 1) % Y) for i in range(Y)]
PERM2 = [(i, (i + 2) % Y if i % 2 == 0 else (i - 2) % Y) for i in range(Y)]
PERM3 = [(i, ((i + 4) ^ 1) % Y) for i in range(Y)]
PAIR = [(i, i ^ 1) for i in range(Y)]
SWAP = [(0, 1), (1, 0)]
VMEM_LIMIT = 40 * 1024 * 1024

VM = pl.BlockSpec(memory_space=pltpu.VMEM)
SM = pl.BlockSpec(memory_space=pltpu.SMEM)
TN = (((0,), (0,)), ((), ()))
NT = (((1,), (1,)), ((), ()))
NN = (((1,), (0,)), ((), ()))


def mm(a, b, dims=NN):
    return lax.dot_general(a, b, dims, preferred_element_type=f32)


def call(kernel, outs, args, flops, moved, n_smem=0, scratch=()):
    return pl.pallas_call(
        kernel,
        out_shape=outs,
        in_specs=[SM] * n_smem + [VM] * (len(args) - n_smem),
        out_specs=jax.tree.map(lambda _: VM, outs),
        scratch_shapes=list(scratch),
        compiler_params=pltpu.CompilerParams(vmem_limit_bytes=VMEM_LIMIT),
        cost_estimate=pl.CostEstimate(flops=flops, bytes_accessed=moved, transcendentals=0),
    )(*args)


def shaped(*shape, dtype=bf16):
    return jax.ShapeDtypeStruct(shape, dtype)


def back_perm(perm):
    return [(b, a) for a, b in perm]


def place_kernel(at, ids, gate, tokens, cotangent, own, one, two, three, placer_out, gate_out):
    y = at[2]
    odd = y % 2
    pair = y // 2
    rows = ids.shape[1]
    e = ids[...]
    expert = lax.broadcasted_iota(jnp.int32, (8, rows), 0)
    onehot = (expert == e).astype(f32)
    before = (
        lax.broadcasted_iota(jnp.int32, (rows, rows), 0)
        < lax.broadcasted_iota(jnp.int32, (rows, rows), 1)
    ).astype(bf16)
    earlier = mm(onehot.astype(bf16), before)
    slot = jnp.sum(onehot * earlier, axis=0, keepdims=True).astype(jnp.int32)
    away = (e - pair + EW) & 3
    near = 1 + 2 * odd
    near = 4 - near
    place = jnp.where(away == 0, 0, jnp.where(away == 2, 3, jnp.where(away == near, 1, 2)))
    target = place * CAP + slot
    placer = (lax.broadcasted_iota(jnp.int32, (rows, rows), 0) == target).astype(f32)
    placed_gate = jnp.sum(placer * gate[...], axis=1, keepdims=True)
    gate_out[...] = jnp.broadcast_to(placed_gate, (rows, rows))
    placer = placer.astype(bf16)
    placer_out[...] = placer
    xs = mm(placer, tokens[...]).astype(bf16)
    ds = (mm(placer, cotangent[...]) * placed_gate).astype(bf16)
    for k, ref in enumerate((own, one, two, three)):
        ref[:, :D] = xs[k * CAP:(k + 1) * CAP]
        ref[:, D:] = ds[k * CAP:(k + 1) * CAP]


def join_kernel(a, b, c, d, out):
    for k, ref in enumerate((a, b, c, d)):
        out[k * CAP:(k + 1) * CAP, :] = ref[...]


def join(parts):
    return call(join_kernel, shaped(4 * CAP, 2 * D), parts, 0, 4 * CAP * 4 * D * 2)


def layer_kernel(touched, mine, mates, wg, wu, wd, out_mine, out_mates, grads):
    expand = (lax.broadcasted_iota(jnp.int32, (TILE, HID), 1) // TILE
              == lax.broadcasted_iota(jnp.int32, (TILE, HID), 0)).astype(f32)
    row = jnp.zeros((TILE, HID), f32)
    for k in range(HID // TILE):
        flag = touched[0, k].astype(f32)
        row = jnp.where(lax.broadcasted_iota(jnp.int32, (TILE, HID), 0) == k, flag, row)
    mask = jnp.sum(expand * row, axis=0, keepdims=True)
    for ref, out, base in ((mine, out_mine, 0), (mates, out_mates, 4 * CAP)):
        xs = ref[:, :D]
        ds = ref[:, D:]
        h = mm(xs, wg[...])
        u = mm(xs, wu[...])
        g = mm(ds, wd[...], NT)
        s = 1.0 / (1.0 + jnp.exp(-h))
        act = (h * s * u).astype(bf16)
        out[...] = mm(act, wd[...]).astype(bf16)
        end = base + 4 * CAP
        grads[base:end, :HID] = (g * u * (s * (1.0 + h * (1.0 - s))) * mask).astype(bf16)
        grads[base:end, HID:2 * HID] = (g * (h * s) * mask).astype(bf16)
        grads[base:end, 2 * HID:] = (act.astype(f32) * mask).astype(bf16)


def layer(touched, mine, mates, wg, wu, wd):
    rows = 8 * CAP
    return call(
        layer_kernel,
        (shaped(4 * CAP, D), shaped(4 * CAP, D), shaped(rows, 3 * HID)),
        (touched, mine, mates, wg, wu, wd),
        2 * 4 * rows * D * HID, 2 * (3 * D * HID + rows * 3 * D), n_smem=1,
    )


STEP = 512


def delta_kernel(at, xa, xb, xc, xd, ga, gb, first, *rest):
    second, held = rest[:Z], rest[Z]
    z = at[1]

    def put(piece, value):
        rep, part = piece // 3, piece % 3
        if part < 2:
            first[rep // Z, rep % Z, part * PART:(part + 1) * PART, :] = value
        else:
            held[lax.rem(rep % Z - z + Z, Z), rep // Z] = value

    grads = jnp.concatenate([ga[...], gb[...]], axis=0)
    for base, lo, n in ((0, 0, 2), (D, 2 * HID, 1)):
        right = grads[:, lo:lo + n * HID]
        for c0 in range(0, D, STEP):
            cols = slice(base + c0, base + c0 + STEP)
            left = jnp.concatenate([r[:, cols] for r in (xa, xb, xc, xd)], axis=0)
            out = mm(left, right, TN).astype(bf16)
            for k in range(n):
                start = ((k if n == 2 else 2) * D + c0) // PART
                for i in range(STEP // PART):
                    put(start + i, out[i * PART:(i + 1) * PART, k * HID:(k + 1) * HID])
    for j in range(Z):
        second[j][...] = held[j]


def delta(at, xs, ga, gb):
    return call(
        delta_kernel,
        (shaped(X, Z, 2 * PART, HID),) + (shaped(X, PART, HID),) * Z,
        (at, *xs, ga, gb),
        2 * 3 * 16 * CAP * D * HID, 2 * (16 * CAP * 2 * D + 3 * D * HID), n_smem=1,
        scratch=(pltpu.VMEM((Z, X, PART, HID), bf16),),
    )


def sum_x_kernel(got, out):
    out[...] = sum(got[k].astype(f32) for k in range(X)).astype(bf16)


def sum_z_kernel(at, *refs):
    x = at[0]
    for j in range(X):
        src = lax.rem(x + j, X)
        refs[Z + j][...] = sum(refs[k][src].astype(f32) for k in range(Z)).astype(bf16)


def last_kernel(got, a, b, c, d, out):
    out[:2 * PART, :] = (sum(got[k].astype(f32) for k in range(Z)) * (1.0 / (X * Z))).astype(bf16)
    out[2 * PART:, :] = (sum(r[...].astype(f32) for r in (a, b, c, d)) * (1.0 / (X * Z))).astype(bf16)


def add_kernel(a, b, out):
    out[...] = (a[...].astype(f32) + b[...].astype(f32)).astype(bf16)


def add_split_kernel(a, b, c, *outs):
    total = (a[...].astype(f32) + b[...].astype(f32) + c[...].astype(f32)).astype(bf16)
    for k in range(4):
        outs[k][...] = total[k * CAP:(k + 1) * CAP]


def mixed_kernel(a, b, c, d, gate, placer, out):
    parts = []
    for k, ref in enumerate((a, b, c, d)):
        parts.append((ref[...].astype(f32) * gate[k * CAP:(k + 1) * CAP, :1]).astype(bf16))
    out[...] = mm(placer[...], jnp.concatenate(parts, axis=0), TN).astype(bf16)


def body(tokens, expert_ids, gate_prob, cotangent, w_gate, w_up, w_down, touched):
    rows = tokens.shape[0]
    at = jnp.stack([lax.axis_index("x"), lax.axis_index("z"), lax.axis_index("y")]).astype(jnp.int32)
    wg, wu, wd = w_gate[0], w_up[0], w_down[0]
    own, one, two, three, placer, gate = call(
        place_kernel,
        (shaped(CAP, 2 * D),) * 4 + (shaped(rows, rows), shaped(rows, rows, dtype=f32)),
        (at, expert_ids.T, gate_prob[None, :], tokens, cotangent),
        2 * 2 * rows * rows * D, 2 * 4 * rows * D, n_smem=1,
    )
    near = [own, lax.ppermute(one, "y", PERM1), lax.ppermute(two, "y", PERM2), lax.ppermute(three, "y", PERM3)]
    far = [lax.ppermute(part, "y", PAIR) for part in near]
    mine = join(near)
    mates = lax.ppermute(mine, "c", SWAP)
    pair_mine = join(far)
    pair_mates = lax.ppermute(pair_mine, "c", SWAP)
    p_mine, p_mates, ga = layer(touched, mine, mates, wg, wu, wd)
    q_mine, q_mates, gb = layer(touched, pair_mine, pair_mates, wg, wu, wd)
    p_got = lax.ppermute(p_mates, "c", SWAP)
    q_got = lax.ppermute(q_mates, "c", SWAP)

    first, *second = delta(at, (mine, mates, pair_mine, pair_mates), ga, gb)
    over_x = lax.all_to_all(first, "x", split_axis=0, concat_axis=0, tiled=True)
    over_z = [second[0]] + [
        lax.ppermute(second[j], "z", [(i, (i + j) % Z) for i in range(Z)]) for j in range(1, Z)
    ]
    sum_x = call(sum_x_kernel, shaped(Z, 2 * PART, HID), (over_x,), 0, 2 * 5 * Z * 2 * PART * HID)
    got = lax.all_to_all(sum_x, "z", split_axis=0, concat_axis=0, tiled=True)
    sums = call(sum_z_kernel, (shaped(PART, HID),) * X, (at, *over_z), 0, 2 * 9 * X * PART * HID, n_smem=1)
    rest = [sums[0]] + [
        lax.ppermute(sums[j], "x", [(i, (i + j) % X) for i in range(X)]) for j in range(1, X)
    ]
    averaged = call(last_kernel, shaped(3 * PART, HID), (got, *rest), 0, 2 * 9 * 3 * PART * HID).T

    q_sum = call(add_kernel, shaped(4 * CAP, D), (q_mine, q_got), 0, 3 * 8 * CAP * D)
    from_pair = lax.ppermute(q_sum, "y", PAIR)
    blocks = call(add_split_kernel, (shaped(CAP, D),) * 4, (p_mine, p_got, from_pair), 0, 4 * 8 * CAP * D)
    back = [blocks[0]] + [
        lax.ppermute(block, "y", back_perm(perm)) for block, perm in zip(blocks[1:], (PERM1, PERM2, PERM3))
    ]
    mixed = call(mixed_kernel, shaped(rows, D), (*back, gate, placer), 2 * rows * rows * D, 2 * 2 * rows * D)
    return mixed, averaged


def solution(mesh):
    fine = Mesh(mesh.devices.reshape(X, Z, Y, C), AXES)
    rep, exp = ("x", "z"), ("y", "c")
    return jax.shard_map(
        body,
        mesh=fine,
        in_specs=(
            P(AXES, None),
            P(AXES, None),
            P(AXES),
            P(AXES, None),
            P(rep, None, exp),
            P(rep, None, exp),
            P(rep, exp, None),
            P(rep, exp),
        ),
        out_specs=(P(AXES, None), P(exp, rep)),
        check_vma=False,
    )
```

```python
import functools

import jax
import jax.numpy as jnp
from jax import lax
from jax.experimental import pallas as pl
from jax.experimental.pallas import tpu as pltpu
from jax.sharding import Mesh, PartitionSpec as P

EW = 4
SHARE = 192
TILE = 16
X, Z, Y, C = 4, 8, 8, 2
AXES = ("x", "z", "y", "c")
CAP = 32
D = 2048
HID = 256
SHARE = 192
bf16 = jnp.bfloat16
f32 = jnp.float32

PERM1 = [(i, (i - 1) % Y if i % 2 == 0 else (i + 1) % Y) for i in range(Y)]
PERM2 = [(i, (i + 2) % Y if i % 2 == 0 else (i - 2) % Y) for i in range(Y)]
PERM3 = [(i, ((i + 4) ^ 1) % Y) for i in range(Y)]
PAIR = [(i, i ^ 1) for i in range(Y)]
SWAP = [(0, 1), (1, 0)]
VMEM_LIMIT = 16 * 1024 * 1024
VMEM_WIDE = 50 * 1024 * 1024
VMEM_WHOLE = 62 * 1024 * 1024

VM = pl.BlockSpec(memory_space=pltpu.VMEM)
SM = pl.BlockSpec(memory_space=pltpu.SMEM)
HB = pl.BlockSpec(memory_space=pl.ANY)
TN = (((0,), (0,)), ((), ()))
NT = (((1,), (1,)), ((), ()))
NN = (((1,), (0,)), ((), ()))


def mm(a, b, dims=NN):
    return lax.dot_general(a, b, dims, preferred_element_type=f32)


class Load:
    def __init__(self, copy, ref):
        self.copy, self.ref, self.waited = copy, ref, False

    def get(self):
        if not self.waited:
            self.copy.wait()
            self.waited = True
        return self.ref


class Store:
    def __init__(self, copy, ref):
        self.copy, self.ref = copy, ref

    def send(self):
        self.copy.start()


def call(kernel, outs, args, flops, moved, space="", out_space="", scratch=(), limit=VMEM_LIMIT):
    single = not isinstance(outs, tuple)
    outs = (outs,) if single else outs
    space = space or "v" * len(args)
    out_space = out_space or "v" * len(outs)
    kind = {"s": SM, "v": VM, "h": HB, "p": HB}
    flat = tuple(args) + outs
    marks = space + out_space
    moving = [i for i, m in enumerate(marks) if m in "hp"]
    parts = outs[0].shape[0] if out_space == "p" else 1
    n_in = len(args)

    def run(*refs):
        main, extra = list(refs[:len(flat)]), refs[len(flat):]
        own, held = extra[:len(scratch)], extra[len(scratch):len(scratch) + len(moving)]
        sems = extra[-1] if moving else None
        loads, stores = [], []
        for k, i in enumerate(moving):
            if i < n_in:
                copy = pltpu.make_async_copy(main[i], held[k], sems.at[k])
                copy.start()
                main[i] = Load(copy, held[k])
                loads.append(main[i])
            elif marks[i] == "h":
                main[i] = Store(pltpu.make_async_copy(held[k], main[i], sems.at[k]), held[k])
                stores.append(main[i])
            else:
                stores = [
                    Store(pltpu.make_async_copy(held[k].at[j], main[i].at[j], sems.at[k + j]), held[k].at[j])
                    for j in range(parts)
                ]
                main[i:] = stores
        kernel(*main, *own)
        for load in loads:
            load.get()
        for store in stores:
            store.copy.wait()

    extra = list(scratch)
    if moving:
        extra += [pltpu.VMEM(flat[i].shape, flat[i].dtype) for i in moving]
        extra.append(pltpu.SemaphoreType.DMA((len(moving) + parts - 1,)))
    got = pl.pallas_call(
        run,
        out_shape=outs,
        in_specs=[kind[m] for m in space],
        out_specs=tuple(kind[m] for m in out_space),
        scratch_shapes=extra,
        compiler_params=pltpu.CompilerParams(vmem_limit_bytes=limit),
        cost_estimate=pl.CostEstimate(flops=flops, bytes_accessed=moved, transcendentals=0),
    )(*args)
    return got[0] if single else got


def shaped(*shape, dtype=bf16):
    return jax.ShapeDtypeStruct(shape, dtype)


def back_perm(perm):
    return [(b, a) for a, b in perm]


def place_kernel(at, ids, gate, tokens, cotangent, own, one, two, three, placer_out, gate_out):
    ids, gate = ids.get(), gate.get()
    y = at[2]
    odd = y % 2
    pair = y // 2
    rows = ids.shape[1]
    e = ids[...]
    expert = lax.broadcasted_iota(jnp.int32, (8, rows), 0)
    onehot = (expert == e).astype(f32)
    before = (
        lax.broadcasted_iota(jnp.int32, (rows, rows), 0)
        < lax.broadcasted_iota(jnp.int32, (rows, rows), 1)
    ).astype(bf16)
    earlier = mm(onehot.astype(bf16), before)
    slot = jnp.sum(onehot * earlier, axis=0, keepdims=True).astype(jnp.int32)
    away = (e - pair + EW) & 3
    near = 1 + 2 * odd
    near = 4 - near
    place = jnp.where(away == 0, 0, jnp.where(away == 2, 3, jnp.where(away == near, 1, 2)))
    target = place * CAP + slot
    placer = (lax.broadcasted_iota(jnp.int32, (rows, rows), 0) == target).astype(f32)
    placed_gate = jnp.sum(placer * gate[...], axis=1, keepdims=True)
    gate_out[...] = jnp.broadcast_to(placed_gate, (rows, rows))
    placer = placer.astype(bf16)
    placer_out[...] = placer
    xs = mm(placer, tokens.get()[...]).astype(bf16)
    ds = (mm(placer, cotangent.get()[...]) * placed_gate).astype(bf16)
    for k, ref in enumerate((own, one, two, three)):
        ref[:, :D] = xs[k * CAP:(k + 1) * CAP]
        ref[:, D:] = ds[k * CAP:(k + 1) * CAP]


def join_kernel(a, b, c, d, out):
    for k, ref in enumerate((a, b, c, d)):
        out[k * CAP:(k + 1) * CAP, :] = ref[...]


def join(parts):
    return call(join_kernel, shaped(4 * CAP, 2 * D), parts, 0, 4 * CAP * 4 * D * 2)


def layer_kernel(n, with_out, touched, *refs):
    blocks, (wg, wu, wd), grads = refs[:n], refs[n:n + 3], refs[n + 3]
    outs = refs[n + 4:]
    row = jnp.zeros((1, HID), f32)
    tile = lax.broadcasted_iota(jnp.int32, (1, HID), 1) // TILE
    for k in range(HID // TILE):
        row = jnp.where(tile == k, touched[0, k].astype(f32), row)
    for k in range(n):
        xs = blocks[k][:, :D]
        ds = blocks[k][:, D:]
        h = mm(xs, wg[...])
        u = mm(xs, wu[...])
        g = mm(ds, wd[...], NT)
        s = 1.0 / (1.0 + jnp.exp(-h))
        act = (h * s * u).astype(bf16)
        here = slice(k * 4 * CAP, (k + 1) * 4 * CAP)
        if with_out:
            outs[k].ref[...] = mm(act, wd[...]).astype(bf16)
            outs[k].send()
        else:
            outs[0][here] = act
        grads[here, :HID] = (g * u * (s * (1.0 + h * (1.0 - s))) * row).astype(bf16)
        grads[here, HID:2 * HID] = (g * (h * s) * row).astype(bf16)
        grads[here, 2 * HID:] = (act.astype(f32) * row).astype(bf16)


def layer(touched, blocks, wg, wu, wd, with_out):
    n = len(blocks)
    rows = n * 4 * CAP
    return call(
        functools.partial(layer_kernel, n, with_out),
        (shaped(rows, 3 * HID),) + ((shaped(4 * CAP, D),) * n if with_out else (shaped(rows, HID),)),
        (touched, *blocks, wg, wu, wd),
        2 * 4 * rows * D * HID, 2 * (3 * D * HID + rows * 3 * D),
        "s" + "v" * (n + 3), "v" + ("h" * n if with_out else "v"),
    )


def out_kernel(mine, mates, wd, out_mine, out_mates):
    out_mates.ref[...] = mm(mates[...], wd[...]).astype(bf16)
    out_mates.send()
    out_mine.ref[...] = mm(mine[...], wd[...]).astype(bf16)
    out_mine.send()


STEP = 512


def delta_kernel(xa, xb, xc, xd, ga, gb, gc, *outs):
    grads = jnp.concatenate([ga[...], gb[...], gc[...]], axis=0)
    left_over = [Z * SHARE] * X
    for base, lo, n in ((0, 0, 2), (D, 2 * HID, 1)):
        right = grads[:, lo:lo + n * HID]
        for c0 in range(0, D, STEP):
            cols = slice(base + c0, base + c0 + STEP)
            left = jnp.concatenate([r[:, cols] for r in (xa, xb, xc, xd)], axis=0)
            out = mm(left, right, TN).astype(bf16)
            for k in range(n):
                start = (k if n == 2 else 2) * D + c0
                for rep in range(start // SHARE, (start + STEP - 1) // SHARE + 1):
                    first = max(rep * SHARE, start)
                    last = min((rep + 1) * SHARE, start + STEP)
                    put = slice(first - rep * SHARE, last - rep * SHARE)
                    x = rep // Z
                    outs[x].ref[rep % Z, put, :] = out[first - start:last - start, k * HID:(k + 1) * HID]
                    left_over[x] -= last - first
                    if left_over[x] == 0:
                        outs[x].send()


def delta(xs, grads):
    return call(
        delta_kernel, shaped(X, Z, SHARE, HID), (*xs, *grads),
        2 * 3 * 16 * CAP * D * HID, 2 * (16 * CAP * 2 * D + 3 * D * HID), "v" * 7, "p", limit=VMEM_WIDE,
    )


ROWS = 64


def fold_kernel(n, chunks, scale, got, out, held, total, in_sems, out_sems):
    per = got.shape[1] // chunks
    loads, stores = [], []
    for c in range(chunks):
        here = pl.ds(c * per, per)
        loads.append(pltpu.make_async_copy(got.at[:, here], held.at[:, here], in_sems.at[c]))
        stores.append(pltpu.make_async_copy(total.at[here], out.at[here], out_sems.at[c]))
        loads[c].start()
    for c in range(chunks):
        loads[c].wait()
        for i in range(c * per, (c + 1) * per):
            value = held[0, i].astype(f32)
            for k in range(1, n):
                value += held[k, i].astype(f32)
            total[i] = (value * scale).astype(bf16)
        stores[c].start()
    for store in stores:
        store.wait()


def fold(got, chunks, scale):
    n = got.shape[0]
    shape = got.shape[1:]
    got = got.reshape(n, -1, ROWS, HID)
    out = pl.pallas_call(
        functools.partial(fold_kernel, n, chunks, scale),
        out_shape=shaped(*got.shape[1:]),
        in_specs=[HB],
        out_specs=HB,
        scratch_shapes=[
            pltpu.VMEM(got.shape, bf16),
            pltpu.VMEM(got.shape[1:], bf16),
            pltpu.SemaphoreType.DMA((chunks,)),
            pltpu.SemaphoreType.DMA((chunks,)),
        ],
        compiler_params=pltpu.CompilerParams(vmem_limit_bytes=VMEM_WHOLE),
        cost_estimate=pl.CostEstimate(flops=0, bytes_accessed=2 * got.size, transcendentals=0),
    )(got)
    return out.reshape(shape)


def add_kernel(a, b, out):
    out.ref[...] = (a[...].astype(f32) + b[...].astype(f32)).astype(bf16)
    out.send()


def add_split_kernel(a, b, c, *outs):
    a, b, c = a.get(), b.get(), c.get()
    for k in range(4):
        here = slice(k * CAP, (k + 1) * CAP)
        outs[k].ref[...] = (a[here].astype(f32) + b[here].astype(f32) + c[here].astype(f32)).astype(bf16)
        outs[k].send()


def mixed_kernel(a, b, c, d, gate, placer, out):
    parts = []
    for k, ref in enumerate((a, b, c, d)):
        parts.append((ref[...].astype(f32) * gate[k * CAP:(k + 1) * CAP, :1]).astype(bf16))
    out[...] = mm(placer[...], jnp.concatenate(parts, axis=0), TN).astype(bf16)


def body(tokens, expert_ids, gate_prob, cotangent, w_gate, w_up, w_down, touched):
    rows = tokens.shape[0]
    at = jnp.stack([lax.axis_index("x"), lax.axis_index("z"), lax.axis_index("y")]).astype(jnp.int32)
    wg, wu, wd = w_gate[0], w_up[0], w_down[0]
    own, one, two, three, placer, gate = call(
        place_kernel,
        (shaped(CAP, 2 * D),) * 4 + (shaped(rows, rows), shaped(rows, rows, dtype=f32)),
        (at, expert_ids.T, gate_prob[None, :], tokens, cotangent),
        2 * 2 * rows * rows * D, 2 * 4 * rows * D, "shhhh", limit=VMEM_WHOLE,
    )
    near = [own, lax.ppermute(one, "y", PERM1), lax.ppermute(two, "y", PERM2), lax.ppermute(three, "y", PERM3)]
    far = [lax.ppermute(part, "y", PAIR) for part in near]
    mine = join(near)
    mates = lax.ppermute(mine, "c", SWAP)
    pair_mine = join(far)
    pair_mates = lax.ppermute(pair_mine, "c", SWAP)
    ga, p_mine, p_mates = layer(touched, (mine, mates), wg, wu, wd, True)
    p_got = lax.ppermute(p_mates, "c", SWAP)
    gb, act_mine = layer(touched, (pair_mine,), wg, wu, wd, False)
    gc, act_mates = layer(touched, (pair_mates,), wg, wu, wd, False)
    deltas = delta((mine, mates, pair_mine, pair_mates), (ga, gb, gc))
    over_x = lax.all_to_all(deltas, "x", split_axis=0, concat_axis=0, tiled=True)
    q_mine, q_mates = call(
        out_kernel, (shaped(4 * CAP, D),) * 2, (act_mine, act_mates, wd), 0, 0, "vvv", "hh"
    )
    q_got = lax.ppermute(q_mates, "c", SWAP)
    q_sum = call(add_kernel, shaped(4 * CAP, D), (q_mine, q_got), 0, 0, "vv", "h")
    from_pair = lax.ppermute(q_sum, "y", PAIR)
    blocks = call(
        add_split_kernel, (shaped(CAP, D),) * 4, (p_mine, p_got, from_pair), 0, 0,
        "hhh", "hhhh", limit=VMEM_WHOLE,
    )
    back = [blocks[0]] + [
        lax.ppermute(block, "y", back_perm(perm)) for block, perm in zip(blocks[1:], (PERM1, PERM2, PERM3))
    ]
    over_x, back[1:3] = lax.optimization_barrier((over_x, back[1:3]))
    got = lax.all_to_all(fold(over_x, 8, 1.0), "z", split_axis=0, concat_axis=0, tiled=True)
    got, back = lax.optimization_barrier((got, back))
    averaged = fold(got, 3, 1.0 / (X * Z)).T
    mixed = call(mixed_kernel, shaped(rows, D), (*back, gate, placer), 2 * rows * rows * D, 2 * 2 * rows * D)
    return mixed, averaged


def solution(mesh):
    fine = Mesh(mesh.devices.reshape(X, Z, Y, C), AXES)
    rep, exp = ("x", "z"), ("y", "c")
    return jax.shard_map(
        body,
        mesh=fine,
        in_specs=(
            P(AXES, None),
            P(AXES, None),
            P(AXES),
            P(AXES, None),
            P(rep, None, exp),
            P(rep, None, exp),
            P(rep, exp, None),
            P(rep, exp),
        ),
        out_specs=(P(AXES, None), P(exp, rep)),
        check_vma=False,
    )
```

```python
import functools

import jax
import jax.numpy as jnp
from jax import lax
from jax.experimental import pallas as pl
from jax.experimental.pallas import tpu as pltpu
from jax.sharding import Mesh, PartitionSpec as P

EW = 4
SHARE = 192
TILE = 16
X, Z, Y, C = 4, 8, 8, 2
AXES = ("x", "z", "y", "c")
CAP = 32
D = 2048
HID = 256
SHARE = 192
bf16 = jnp.bfloat16
f32 = jnp.float32

PERM1 = [(i, (i - 1) % Y if i % 2 == 0 else (i + 1) % Y) for i in range(Y)]
PERM2 = [(i, (i + 2) % Y if i % 2 == 0 else (i - 2) % Y) for i in range(Y)]
PERM3 = [(i, ((i + 4) ^ 1) % Y) for i in range(Y)]
PAIR = [(i, i ^ 1) for i in range(Y)]
SWAP = [(0, 1), (1, 0)]
VMEM_LIMIT = 16 * 1024 * 1024
VMEM_WIDE = 50 * 1024 * 1024
VMEM_WHOLE = 62 * 1024 * 1024

VM = pl.BlockSpec(memory_space=pltpu.VMEM)
SM = pl.BlockSpec(memory_space=pltpu.SMEM)
HB = pl.BlockSpec(memory_space=pl.ANY)
TN = (((0,), (0,)), ((), ()))
NT = (((1,), (1,)), ((), ()))
NN = (((1,), (0,)), ((), ()))


def mm(a, b, dims=NN):
    return lax.dot_general(a, b, dims, preferred_element_type=f32)


class Load:
    def __init__(self, copy, ref):
        self.copy, self.ref, self.waited = copy, ref, False

    def get(self):
        if not self.waited:
            self.copy.wait()
            self.waited = True
        return self.ref


class Store:
    def __init__(self, copy, ref):
        self.copy, self.ref = copy, ref

    def send(self):
        self.copy.start()


def call(kernel, outs, args, flops, moved, space="", out_space="", scratch=(), limit=VMEM_LIMIT):
    single = not isinstance(outs, tuple)
    outs = (outs,) if single else outs
    space = space or "v" * len(args)
    out_space = out_space or "v" * len(outs)
    kind = {"s": SM, "v": VM, "h": HB, "p": HB}
    flat = tuple(args) + outs
    marks = space + out_space
    moving = [i for i, m in enumerate(marks) if m in "hp"]
    parts = outs[0].shape[0] if out_space == "p" else 1
    n_in = len(args)

    def run(*refs):
        main, extra = list(refs[:len(flat)]), refs[len(flat):]
        own, held = extra[:len(scratch)], extra[len(scratch):len(scratch) + len(moving)]
        sems = extra[-1] if moving else None
        loads, stores = [], []
        for k, i in enumerate(moving):
            if i < n_in:
                copy = pltpu.make_async_copy(main[i], held[k], sems.at[k])
                copy.start()
                main[i] = Load(copy, held[k])
                loads.append(main[i])
            elif marks[i] == "h":
                main[i] = Store(pltpu.make_async_copy(held[k], main[i], sems.at[k]), held[k])
                stores.append(main[i])
            else:
                stores = [
                    Store(pltpu.make_async_copy(held[k].at[j], main[i].at[j], sems.at[k + j]), held[k].at[j])
                    for j in range(parts)
                ]
                main[i:] = stores
        kernel(*main, *own)
        for load in loads:
            load.get()
        for store in stores:
            store.copy.wait()

    extra = list(scratch)
    if moving:
        extra += [pltpu.VMEM(flat[i].shape, flat[i].dtype) for i in moving]
        extra.append(pltpu.SemaphoreType.DMA((len(moving) + parts - 1,)))
    got = pl.pallas_call(
        run,
        out_shape=outs,
        in_specs=[kind[m] for m in space],
        out_specs=tuple(kind[m] for m in out_space),
        scratch_shapes=extra,
        compiler_params=pltpu.CompilerParams(vmem_limit_bytes=limit),
        cost_estimate=pl.CostEstimate(flops=flops, bytes_accessed=moved, transcendentals=0),
    )(*args)
    return got[0] if single else got


def shaped(*shape, dtype=bf16):
    return jax.ShapeDtypeStruct(shape, dtype)


def back_perm(perm):
    return [(b, a) for a, b in perm]


def place_kernel(at, ids, gate, tokens, cotangent, own, one, two, three, placer_out, gate_out):
    ids, gate = ids.get(), gate.get()
    y = at[2]
    odd = y % 2
    pair = y // 2
    rows = ids.shape[1]
    e = ids[...]
    expert = lax.broadcasted_iota(jnp.int32, (8, rows), 0)
    onehot = (expert == e).astype(f32)
    before = (
        lax.broadcasted_iota(jnp.int32, (rows, rows), 0)
        < lax.broadcasted_iota(jnp.int32, (rows, rows), 1)
    ).astype(bf16)
    earlier = mm(onehot.astype(bf16), before)
    slot = jnp.sum(onehot * earlier, axis=0, keepdims=True).astype(jnp.int32)
    away = (e - pair + EW) & 3
    near = 1 + 2 * odd
    near = 4 - near
    place = jnp.where(away == 0, 0, jnp.where(away == 2, 3, jnp.where(away == near, 1, 2)))
    target = place * CAP + slot
    placer = (lax.broadcasted_iota(jnp.int32, (rows, rows), 0) == target).astype(f32)
    placed_gate = jnp.sum(placer * gate[...], axis=1, keepdims=True)
    gate_out[...] = jnp.broadcast_to(placed_gate, (rows, rows))
    placer = placer.astype(bf16)
    placer_out[...] = placer
    xs = mm(placer, tokens.get()[...]).astype(bf16)
    ds = (mm(placer, cotangent.get()[...]) * placed_gate).astype(bf16)
    for k, ref in enumerate((own, one, two, three)):
        ref[:, :D] = xs[k * CAP:(k + 1) * CAP]
        ref[:, D:] = ds[k * CAP:(k + 1) * CAP]


def join_kernel(a, b, c, d, out):
    for k, ref in enumerate((a, b, c, d)):
        out[k * CAP:(k + 1) * CAP, :] = ref[...]


def join(parts):
    return call(join_kernel, shaped(4 * CAP, 2 * D), parts, 0, 4 * CAP * 4 * D * 2)


def layer_kernel(n, with_out, touched, *refs):
    blocks, (wg, wu, wd), grads = refs[:n], refs[n:n + 3], refs[n + 3]
    outs = refs[n + 4:]
    row = jnp.zeros((1, HID), f32)
    tile = lax.broadcasted_iota(jnp.int32, (1, HID), 1) // TILE
    for k in range(HID // TILE):
        row = jnp.where(tile == k, touched[0, k].astype(f32), row)
    for k in range(n):
        xs = blocks[k][:, :D]
        ds = blocks[k][:, D:]
        h = mm(xs, wg[...])
        u = mm(xs, wu[...])
        g = mm(ds, wd[...], NT)
        s = 1.0 / (1.0 + jnp.exp(-h))
        act = (h * s * u).astype(bf16)
        here = slice(k * 4 * CAP, (k + 1) * 4 * CAP)
        if with_out:
            outs[k].ref[...] = mm(act, wd[...]).astype(bf16)
            outs[k].send()
        else:
            outs[0][here] = act
        grads[here, :HID] = (g * u * (s * (1.0 + h * (1.0 - s))) * row).astype(bf16)
        grads[here, HID:2 * HID] = (g * (h * s) * row).astype(bf16)
        grads[here, 2 * HID:] = (act.astype(f32) * row).astype(bf16)


def layer(touched, blocks, wg, wu, wd, with_out):
    n = len(blocks)
    rows = n * 4 * CAP
    return call(
        functools.partial(layer_kernel, n, with_out),
        (shaped(rows, 3 * HID),) + ((shaped(4 * CAP, D),) * n if with_out else (shaped(rows, HID),)),
        (touched, *blocks, wg, wu, wd),
        2 * 4 * rows * D * HID, 2 * (3 * D * HID + rows * 3 * D),
        "s" + "v" * (n + 3), "v" + ("h" * n if with_out else "v"),
    )


def out_kernel(mine, mates, wd, out_mine, out_mates):
    out_mates.ref[...] = mm(mates[...], wd[...]).astype(bf16)
    out_mates.send()
    out_mine.ref[...] = mm(mine[...], wd[...]).astype(bf16)
    out_mine.send()


STEP = 512


def delta_kernel(xa, xb, xc, xd, ga, gb, gc, *outs):
    grads = jnp.concatenate([ga[...], gb[...], gc[...]], axis=0)
    left_over = [Z * SHARE] * X
    for base, lo, n in ((0, 0, 2), (D, 2 * HID, 1)):
        right = grads[:, lo:lo + n * HID]
        for c0 in range(0, D, STEP):
            cols = slice(base + c0, base + c0 + STEP)
            left = jnp.concatenate([r[:, cols] for r in (xa, xb, xc, xd)], axis=0)
            out = mm(left, right, TN).astype(bf16)
            for k in range(n):
                start = (k if n == 2 else 2) * D + c0
                for rep in range(start // SHARE, (start + STEP - 1) // SHARE + 1):
                    first = max(rep * SHARE, start)
                    last = min((rep + 1) * SHARE, start + STEP)
                    put = slice(first - rep * SHARE, last - rep * SHARE)
                    x = rep // Z
                    outs[x].ref[rep % Z, put, :] = out[first - start:last - start, k * HID:(k + 1) * HID]
                    left_over[x] -= last - first
                    if left_over[x] == 0:
                        outs[x].send()


def delta(xs, grads):
    return call(
        delta_kernel, shaped(X, Z, SHARE, HID), (*xs, *grads),
        2 * 3 * 16 * CAP * D * HID, 2 * (16 * CAP * 2 * D + 3 * D * HID), "v" * 7, "p", limit=VMEM_WIDE,
    )


ROWS = 64


def fold_kernel(n, chunks, scale, got, out, total, sems):
    per = got.shape[1] // chunks
    stores = []
    for c in range(chunks):
        for i in range(c * per, (c + 1) * per):
            value = got[0, i].astype(f32)
            for k in range(1, n):
                value += got[k, i].astype(f32)
            total[i] = (value * scale).astype(bf16)
        here = pl.ds(c * per, per)
        stores.append(pltpu.make_async_copy(total.at[here], out.at[here], sems.at[c]))
        stores[c].start()
    for store in stores:
        store.wait()


def fold(got, chunks, scale):
    n = got.shape[0]
    shape = got.shape[1:]
    got = got.reshape(n, -1, ROWS, HID)
    out = pl.pallas_call(
        functools.partial(fold_kernel, n, chunks, scale),
        out_shape=shaped(*got.shape[1:]),
        in_specs=[VM],
        out_specs=HB,
        scratch_shapes=[pltpu.VMEM(got.shape[1:], bf16), pltpu.SemaphoreType.DMA((chunks,))],
        compiler_params=pltpu.CompilerParams(vmem_limit_bytes=VMEM_WIDE),
        cost_estimate=pl.CostEstimate(flops=0, bytes_accessed=2 * got.size, transcendentals=0),
    )(got)
    return out.reshape(shape)


def add_kernel(a, b, out):
    out.ref[...] = (a[...].astype(f32) + b[...].astype(f32)).astype(bf16)
    out.send()


def add_split_kernel(a, b, c, *outs):
    for k in range(4):
        here = slice(k * CAP, (k + 1) * CAP)
        outs[k].ref[...] = (a[here].astype(f32) + b[here].astype(f32) + c[here].astype(f32)).astype(bf16)
        outs[k].send()


def mixed_kernel(a, b, c, d, gate, placer, out):
    parts = []
    for k, ref in enumerate((a, b, c, d)):
        parts.append((ref[...].astype(f32) * gate[k * CAP:(k + 1) * CAP, :1]).astype(bf16))
    out[...] = mm(placer[...], jnp.concatenate(parts, axis=0), TN).astype(bf16)


def body(tokens, expert_ids, gate_prob, cotangent, w_gate, w_up, w_down, touched):
    rows = tokens.shape[0]
    at = jnp.stack([lax.axis_index("x"), lax.axis_index("z"), lax.axis_index("y")]).astype(jnp.int32)
    wg, wu, wd = w_gate[0], w_up[0], w_down[0]
    own, one, two, three, placer, gate = call(
        place_kernel,
        (shaped(CAP, 2 * D),) * 4 + (shaped(rows, rows), shaped(rows, rows, dtype=f32)),
        (at, expert_ids.T, gate_prob[None, :], tokens, cotangent),
        2 * 2 * rows * rows * D, 2 * 4 * rows * D, "shhhh", limit=VMEM_WHOLE,
    )
    near = [own, lax.ppermute(one, "y", PERM1), lax.ppermute(two, "y", PERM2), lax.ppermute(three, "y", PERM3)]
    far = [lax.ppermute(part, "y", PAIR) for part in near]
    mine = join(near)
    mates = lax.ppermute(mine, "c", SWAP)
    pair_mine = join(far)
    pair_mates = lax.ppermute(pair_mine, "c", SWAP)
    ga, p_mine, p_mates = layer(touched, (mine, mates), wg, wu, wd, True)
    p_got = lax.ppermute(p_mates, "c", SWAP)
    gc, act_mine = layer(touched, (pair_mine,), wg, wu, wd, False)
    gd, act_mates = layer(touched, (pair_mates,), wg, wu, wd, False)

    deltas = delta((mine, mates, pair_mine, pair_mates), (ga, gc, gd))
    over_x = lax.all_to_all(deltas, "x", split_axis=0, concat_axis=0, tiled=True)
    q_mine, q_mates = call(
        out_kernel, (shaped(4 * CAP, D),) * 2, (act_mine, act_mates, wd), 0, 0, "vvv", "hh"
    )
    q_got = lax.ppermute(q_mates, "c", SWAP)
    q_sum = call(add_kernel, shaped(4 * CAP, D), (q_mine, q_got), 0, 0, "vv", "h")
    from_pair = lax.ppermute(q_sum, "y", PAIR)
    blocks = call(
        add_split_kernel, (shaped(CAP, D),) * 4, (p_mine, p_got, from_pair), 0, 0,
        "vvv", "hhhh", limit=VMEM_WIDE,
    )
    back = [blocks[0]] + [
        lax.ppermute(block, "y", back_perm(perm)) for block, perm in zip(blocks[1:], (PERM1, PERM2, PERM3))
    ]
    over_x, back[1:3] = lax.optimization_barrier((over_x, back[1:3]))
    got = lax.all_to_all(fold(over_x, 8, 1.0), "z", split_axis=0, concat_axis=0, tiled=True)
    mixed = call(mixed_kernel, shaped(rows, D), (*back, gate, placer), 2 * rows * rows * D, 2 * 2 * rows * D)
    got, mixed = lax.optimization_barrier((got, mixed))
    averaged = fold(got, 3, 1.0 / (X * Z)).T
    return mixed, averaged


def solution(mesh):
    fine = Mesh(mesh.devices.reshape(X, Z, Y, C), AXES)
    rep, exp = ("x", "z"), ("y", "c")
    return jax.shard_map(
        body,
        mesh=fine,
        in_specs=(
            P(AXES, None),
            P(AXES, None),
            P(AXES),
            P(AXES, None),
            P(rep, None, exp),
            P(rep, None, exp),
            P(rep, exp, None),
            P(rep, exp),
        ),
        out_specs=(P(AXES, None), P(exp, rep)),
        check_vma=False,
    )
```

```python
import functools

import jax
import jax.numpy as jnp
from jax import lax
from jax.experimental import pallas as pl
from jax.experimental.pallas import tpu as pltpu
from jax.sharding import Mesh, PartitionSpec as P

EW = 4
SHARE = 192
TILE = 16
X, Z, Y, C = 4, 8, 8, 2
AXES = ("x", "z", "y", "c")
CAP = 32
D = 2048
HID = 256
SHARE = 192
bf16 = jnp.bfloat16
f32 = jnp.float32

PERM1 = [(i, (i - 1) % Y if i % 2 == 0 else (i + 1) % Y) for i in range(Y)]
PERM2 = [(i, (i + 2) % Y if i % 2 == 0 else (i - 2) % Y) for i in range(Y)]
PERM3 = [(i, ((i + 4) ^ 1) % Y) for i in range(Y)]
PAIR = [(i, i ^ 1) for i in range(Y)]
SWAP = [(0, 1), (1, 0)]
VMEM_LIMIT = 16 * 1024 * 1024
VMEM_WIDE = 50 * 1024 * 1024
VMEM_WHOLE = 62 * 1024 * 1024

VM = pl.BlockSpec(memory_space=pltpu.VMEM)
SM = pl.BlockSpec(memory_space=pltpu.SMEM)
HB = pl.BlockSpec(memory_space=pl.ANY)
TN = (((0,), (0,)), ((), ()))
NT = (((1,), (1,)), ((), ()))
NN = (((1,), (0,)), ((), ()))


def mm(a, b, dims=NN):
    return lax.dot_general(a, b, dims, preferred_element_type=f32)


class Load:
    def __init__(self, copy, ref):
        self.copy, self.ref, self.waited = copy, ref, False

    def get(self):
        if not self.waited:
            self.copy.wait()
            self.waited = True
        return self.ref


class Store:
    def __init__(self, copy, ref):
        self.copy, self.ref = copy, ref

    def send(self):
        self.copy.start()


def call(kernel, outs, args, flops, moved, space="", out_space="", scratch=(), limit=VMEM_LIMIT):
    single = not isinstance(outs, tuple)
    outs = (outs,) if single else outs
    space = space or "v" * len(args)
    out_space = out_space or "v" * len(outs)
    kind = {"s": SM, "v": VM, "h": HB, "p": HB}
    flat = tuple(args) + outs
    marks = space + out_space
    moving = [i for i, m in enumerate(marks) if m in "hp"]
    parts = outs[0].shape[0] if out_space == "p" else 1
    n_in = len(args)

    def run(*refs):
        main, extra = list(refs[:len(flat)]), refs[len(flat):]
        own, held = extra[:len(scratch)], extra[len(scratch):len(scratch) + len(moving)]
        sems = extra[-1] if moving else None
        loads, stores = [], []
        for k, i in enumerate(moving):
            if i < n_in:
                copy = pltpu.make_async_copy(main[i], held[k], sems.at[k])
                copy.start()
                main[i] = Load(copy, held[k])
                loads.append(main[i])
            elif marks[i] == "h":
                main[i] = Store(pltpu.make_async_copy(held[k], main[i], sems.at[k]), held[k])
                stores.append(main[i])
            else:
                stores = [
                    Store(pltpu.make_async_copy(held[k].at[j], main[i].at[j], sems.at[k + j]), held[k].at[j])
                    for j in range(parts)
                ]
                main[i:] = stores
        kernel(*main, *own)
        for load in loads:
            load.get()
        for store in stores:
            store.copy.wait()

    extra = list(scratch)
    if moving:
        extra += [pltpu.VMEM(flat[i].shape, flat[i].dtype) for i in moving]
        extra.append(pltpu.SemaphoreType.DMA((len(moving) + parts - 1,)))
    got = pl.pallas_call(
        run,
        out_shape=outs,
        in_specs=[kind[m] for m in space],
        out_specs=tuple(kind[m] for m in out_space),
        scratch_shapes=extra,
        compiler_params=pltpu.CompilerParams(vmem_limit_bytes=limit),
        cost_estimate=pl.CostEstimate(flops=flops, bytes_accessed=moved, transcendentals=0),
    )(*args)
    return got[0] if single else got


def shaped(*shape, dtype=bf16):
    return jax.ShapeDtypeStruct(shape, dtype)


def back_perm(perm):
    return [(b, a) for a, b in perm]


def place_kernel(at, ids, gate, tokens, cotangent, own, one, two, three, placer_out, gate_out):
    ids, gate = ids.get(), gate.get()
    y = at[0]
    odd = y % 2
    pair = y // 2
    rows = ids.shape[1]
    e = ids[...]
    expert = lax.broadcasted_iota(jnp.int32, (8, rows), 0)
    onehot = (expert == e).astype(f32)
    before = (
        lax.broadcasted_iota(jnp.int32, (rows, rows), 0)
        < lax.broadcasted_iota(jnp.int32, (rows, rows), 1)
    ).astype(bf16)
    earlier = mm(onehot.astype(bf16), before)
    slot = jnp.sum(onehot * earlier, axis=0, keepdims=True).astype(jnp.int32)
    away = (e - pair + EW) & 3
    near = 1 + 2 * odd
    near = 4 - near
    place = jnp.where(away == 0, 0, jnp.where(away == 2, 3, jnp.where(away == near, 1, 2)))
    target = place * CAP + slot
    placer = (lax.broadcasted_iota(jnp.int32, (rows, rows), 0) == target).astype(f32)
    placed_gate = jnp.sum(placer * gate[...], axis=1, keepdims=True)
    gate_out[...] = jnp.broadcast_to(placed_gate, (rows, rows))
    placer = placer.astype(bf16)
    placer_out[...] = placer
    xs = mm(placer, tokens.get()[...]).astype(bf16)
    ds = (mm(placer, cotangent.get()[...]) * placed_gate).astype(bf16)
    for k, ref in enumerate((own, one, two, three)):
        ref[:, :D] = xs[k * CAP:(k + 1) * CAP]
        ref[:, D:] = ds[k * CAP:(k + 1) * CAP]


def join_kernel(a, b, c, d, out):
    for k, ref in enumerate((a, b, c, d)):
        out[k * CAP:(k + 1) * CAP, :] = ref[...]


def join(parts):
    return call(join_kernel, shaped(4 * CAP, 2 * D), parts, 0, 4 * CAP * 4 * D * 2)


def layer_kernel(n, with_out, touched, *refs):
    blocks, (wg, wu, wd), grads = refs[:n], refs[n:n + 3], refs[n + 3]
    outs = refs[n + 4:]
    row = jnp.zeros((1, HID), f32)
    tile = lax.broadcasted_iota(jnp.int32, (1, HID), 1) // TILE
    for k in range(HID // TILE):
        row = jnp.where(tile == k, touched[0, k].astype(f32), row)
    xs = jnp.concatenate([block[:, :D] for block in blocks], axis=0)
    ds = jnp.concatenate([block[:, D:] for block in blocks], axis=0)
    h = mm(xs, wg[...])
    u = mm(xs, wu[...])
    g = mm(ds, wd[...], NT)
    s = 1.0 / (1.0 + jnp.exp(-h))
    act = (h * s * u).astype(bf16)
    if with_out:
        made = mm(act, wd[...]).astype(bf16)
        for k in range(n):
            outs[k].ref[...] = made[k * 4 * CAP:(k + 1) * 4 * CAP]
            outs[k].send()
    else:
        outs[0][...] = act
    grads[:, :HID] = (g * u * (s * (1.0 + h * (1.0 - s))) * row).astype(bf16)
    grads[:, HID:2 * HID] = (g * (h * s) * row).astype(bf16)
    grads[:, 2 * HID:] = (act.astype(f32) * row).astype(bf16)


def layer(touched, blocks, wg, wu, wd, with_out):
    n = len(blocks)
    rows = n * 4 * CAP
    return call(
        functools.partial(layer_kernel, n, with_out),
        (shaped(rows, 3 * HID),) + ((shaped(4 * CAP, D),) * n if with_out else (shaped(rows, HID),)),
        (touched, *blocks, wg, wu, wd),
        2 * 4 * rows * D * HID, 2 * (3 * D * HID + rows * 3 * D),
        "s" + "v" * (n + 3), "v" + ("h" * n if with_out else "v"),
    )


def out_kernel(mine, mates, wd, out_mine, out_mates):
    out_mates.ref[...] = mm(mates[...], wd[...]).astype(bf16)
    out_mates.send()
    out_mine.ref[...] = mm(mine[...], wd[...]).astype(bf16)
    out_mine.send()


STEP = 512


PAIRED = 2


def delta_kernel(xa, xb, xc, xd, ga, gb, gc, *outs):
    grads = jnp.concatenate([ga[...], gb[...], gc[...]], axis=0)
    left_over = [PAIRED * SHARE] * len(outs)
    for base, lo, n in ((0, 0, 2), (D, 2 * HID, 1)):
        right = grads[:, lo:lo + n * HID]
        for c0 in range(0, D, STEP):
            cols = slice(base + c0, base + c0 + STEP)
            left = jnp.concatenate([r[:, cols] for r in (xa, xb, xc, xd)], axis=0)
            out = mm(left, right, TN).astype(bf16)
            for k in range(n):
                start = (k if n == 2 else 2) * D + c0
                for rep in range(start // SHARE, (start + STEP - 1) // SHARE + 1):
                    first = max(rep * SHARE, start)
                    last = min((rep + 1) * SHARE, start + STEP)
                    part, off = rep // PAIRED, (rep // PAIRED) * PAIRED * SHARE
                    put = slice(first - off, last - off)
                    outs[part].ref[put, :] = out[first - start:last - start, k * HID:(k + 1) * HID]
                    left_over[part] -= last - first
                    if left_over[part] == 0:
                        outs[part].send()


def delta(xs, grads):
    out = call(
        delta_kernel, shaped(X * Z // PAIRED, PAIRED * SHARE, HID), (*xs, *grads),
        2 * 3 * 16 * CAP * D * HID, 2 * (16 * CAP * 2 * D + 3 * D * HID), "v" * 7, "p", limit=VMEM_WIDE,
    )
    return out.reshape(X, Z, SHARE, HID)


ROWS = 64


def fold_kernel(n, chunks, scale, staged, got, out, total, sems, *rest):
    per = got.shape[1] // chunks
    parts = [pl.ds(c * per, per) for c in range(chunks)]
    stores, loads = [], []
    if staged:
        held, in_sems = rest
        for c, here in enumerate(parts):
            loads.append(pltpu.make_async_copy(got.at[:, here], held.at[:, here], in_sems.at[c]))
            loads[c].start()
        got = held
    for c, here in enumerate(parts):
        if staged:
            loads[c].wait()
        for i in range(c * per, (c + 1) * per):
            value = got[0, i].astype(f32)
            for k in range(1, n):
                value += got[k, i].astype(f32)
            total[i] = (value * scale).astype(bf16)
        stores.append(pltpu.make_async_copy(total.at[here], out.at[here], sems.at[c]))
        stores[c].start()
    for store in stores:
        store.wait()


def fold(got, chunks, scale, staged):
    n = got.shape[0]
    shape = got.shape[1:]
    got = got.reshape(n, -1, ROWS, HID)
    scratch = [pltpu.VMEM(got.shape[1:], bf16), pltpu.SemaphoreType.DMA((chunks,))]
    if staged:
        scratch += [pltpu.VMEM(got.shape, bf16), pltpu.SemaphoreType.DMA((chunks,))]
    out = pl.pallas_call(
        functools.partial(fold_kernel, n, chunks, scale, staged),
        out_shape=shaped(*got.shape[1:]),
        in_specs=[HB if staged else VM],
        out_specs=HB,
        scratch_shapes=scratch,
        compiler_params=pltpu.CompilerParams(vmem_limit_bytes=VMEM_WHOLE if staged else VMEM_WIDE),
        cost_estimate=pl.CostEstimate(flops=0, bytes_accessed=2 * got.size, transcendentals=0),
    )(got)
    return out.reshape(shape)


def add_kernel(a, b, out):
    out.ref[...] = (a[...].astype(f32) + b[...].astype(f32)).astype(bf16)
    out.send()


def add_split_kernel(a, b, c, *outs):
    for k in range(4):
        here = slice(k * CAP, (k + 1) * CAP)
        outs[k].ref[...] = (a[here].astype(f32) + b[here].astype(f32) + c[here].astype(f32)).astype(bf16)
        outs[k].send()


def mixed_kernel(a, b, c, d, gate, placer, out):
    parts = []
    for k, ref in enumerate((a, b, c, d)):
        parts.append((ref[...].astype(f32) * gate[k * CAP:(k + 1) * CAP, :1]).astype(bf16))
    out[...] = mm(placer[...], jnp.concatenate(parts, axis=0), TN).astype(bf16)


def body(tokens, expert_ids, gate_prob, cotangent, w_gate, w_up, w_down, touched):
    rows = tokens.shape[0]
    at = lax.axis_index("y").astype(jnp.int32).reshape(1)
    wg, wu, wd = w_gate[0], w_up[0], w_down[0]
    own, one, two, three, placer, gate = call(
        place_kernel,
        (shaped(CAP, 2 * D),) * 4 + (shaped(rows, rows), shaped(rows, rows, dtype=f32)),
        (at, expert_ids.T, gate_prob[None, :], tokens, cotangent),
        2 * 2 * rows * rows * D, 2 * 4 * rows * D, "shhhh", limit=VMEM_WHOLE,
    )
    near = [own, lax.ppermute(one, "y", PERM1), lax.ppermute(two, "y", PERM2), lax.ppermute(three, "y", PERM3)]
    far = [lax.ppermute(part, "y", PAIR) for part in near]
    mine = join(near)
    mates = lax.ppermute(mine, "c", SWAP)
    pair_mine = join(far)
    pair_mates = lax.ppermute(pair_mine, "c", SWAP)
    ga, p_mine, p_mates = layer(touched, (mine, mates), wg, wu, wd, True)
    p_got = lax.ppermute(p_mates, "c", SWAP)
    gc, act_mine = layer(touched, (pair_mine,), wg, wu, wd, False)
    gd, act_mates = layer(touched, (pair_mates,), wg, wu, wd, False)

    deltas = delta((mine, mates, pair_mine, pair_mates), (ga, gc, gd))
    over_x = lax.all_to_all(deltas, "x", split_axis=0, concat_axis=0, tiled=True)
    q_mine, q_mates = call(
        out_kernel, (shaped(4 * CAP, D),) * 2, (act_mine, act_mates, wd), 0, 0, "vvv", "hh"
    )
    q_got = lax.ppermute(q_mates, "c", SWAP)
    q_sum = call(add_kernel, shaped(4 * CAP, D), (q_mine, q_got), 0, 0, "vv", "h")
    from_pair = lax.ppermute(q_sum, "y", PAIR)
    blocks = call(
        add_split_kernel, (shaped(CAP, D),) * 4, (p_mine, p_got, from_pair), 0, 0,
        "vvv", "hhhh", limit=VMEM_WIDE,
    )
    back = [blocks[0]] + [
        lax.ppermute(block, "y", back_perm(perm)) for block, perm in zip(blocks[1:], (PERM1, PERM2, PERM3))
    ]
    over_x, back[1:3] = lax.optimization_barrier((over_x, back[1:3]))
    got = lax.all_to_all(fold(over_x, 8, 1.0, True), "z", split_axis=0, concat_axis=0, tiled=True)
    mixed = call(mixed_kernel, shaped(rows, D), (*back, gate, placer), 2 * rows * rows * D, 2 * 2 * rows * D)
    got, mixed = lax.optimization_barrier((got, mixed))
    averaged = fold(got, 3, 1.0 / (X * Z), False).T
    return mixed, averaged


def solution(mesh):
    fine = Mesh(mesh.devices.reshape(X, Z, Y, C), AXES)
    rep, exp = ("x", "z"), ("y", "c")
    return jax.shard_map(
        body,
        mesh=fine,
        in_specs=(
            P(AXES, None),
            P(AXES, None),
            P(AXES),
            P(AXES, None),
            P(rep, None, exp),
            P(rep, None, exp),
            P(rep, exp, None),
            P(rep, exp),
        ),
        out_specs=(P(AXES, None), P(exp, rep)),
        check_vma=False,
    )
```

```python
import functools

import jax
import jax.numpy as jnp
from jax import lax
from jax.experimental import pallas as pl
from jax.experimental.pallas import tpu as pltpu
from jax.sharding import Mesh, PartitionSpec as P

EW = 4
SHARE = 192
TILE = 16
X, Z, Y, C = 4, 8, 8, 2
AXES = ("x", "z", "y", "c")
CAP = 32
D = 2048
HID = 256
SHARE = 192
bf16 = jnp.bfloat16
f32 = jnp.float32

PERM1 = [(i, (i - 1) % Y if i % 2 == 0 else (i + 1) % Y) for i in range(Y)]
PERM2 = [(i, (i + 2) % Y if i % 2 == 0 else (i - 2) % Y) for i in range(Y)]
PERM3 = [(i, ((i + 4) ^ 1) % Y) for i in range(Y)]
PAIR = [(i, i ^ 1) for i in range(Y)]
SWAP = [(0, 1), (1, 0)]
VMEM_LIMIT = 16 * 1024 * 1024
VMEM_WIDE = 50 * 1024 * 1024
VMEM_WHOLE = 62 * 1024 * 1024

VM = pl.BlockSpec(memory_space=pltpu.VMEM)
SM = pl.BlockSpec(memory_space=pltpu.SMEM)
HB = pl.BlockSpec(memory_space=pl.ANY)
TN = (((0,), (0,)), ((), ()))
NT = (((1,), (1,)), ((), ()))
NN = (((1,), (0,)), ((), ()))


def mm(a, b, dims=NN):
    return lax.dot_general(a, b, dims, preferred_element_type=f32)


class Load:
    def __init__(self, copy, ref):
        self.copy, self.ref, self.waited = copy, ref, False

    def get(self):
        if not self.waited:
            self.copy.wait()
            self.waited = True
        return self.ref


class Store:
    def __init__(self, copy, ref):
        self.copy, self.ref = copy, ref

    def send(self):
        self.copy.start()


def call(kernel, outs, args, flops, moved, space="", out_space="", scratch=(), limit=VMEM_LIMIT):
    single = not isinstance(outs, tuple)
    outs = (outs,) if single else outs
    space = space or "v" * len(args)
    out_space = out_space or "v" * len(outs)
    kind = {"s": SM, "v": VM, "h": HB, "p": HB}
    flat = tuple(args) + outs
    marks = space + out_space
    moving = [i for i, m in enumerate(marks) if m in "hp"]
    parts = outs[0].shape[0] if out_space == "p" else 1
    n_in = len(args)

    def run(*refs):
        main, extra = list(refs[:len(flat)]), refs[len(flat):]
        own, held = extra[:len(scratch)], extra[len(scratch):len(scratch) + len(moving)]
        sems = extra[-1] if moving else None
        loads, stores = [], []
        for k, i in enumerate(moving):
            if i < n_in:
                copy = pltpu.make_async_copy(main[i], held[k], sems.at[k])
                copy.start()
                main[i] = Load(copy, held[k])
                loads.append(main[i])
            elif marks[i] == "h":
                main[i] = Store(pltpu.make_async_copy(held[k], main[i], sems.at[k]), held[k])
                stores.append(main[i])
            else:
                stores = [
                    Store(pltpu.make_async_copy(held[k].at[j], main[i].at[j], sems.at[k + j]), held[k].at[j])
                    for j in range(parts)
                ]
                main[i:] = stores
        kernel(*main, *own)
        for load in loads:
            load.get()
        for store in stores:
            store.copy.wait()

    extra = list(scratch)
    if moving:
        extra += [pltpu.VMEM(flat[i].shape, flat[i].dtype) for i in moving]
        extra.append(pltpu.SemaphoreType.DMA((len(moving) + parts - 1,)))
    got = pl.pallas_call(
        run,
        out_shape=outs,
        in_specs=[kind[m] for m in space],
        out_specs=tuple(kind[m] for m in out_space),
        scratch_shapes=extra,
        compiler_params=pltpu.CompilerParams(vmem_limit_bytes=limit),
        cost_estimate=pl.CostEstimate(flops=flops, bytes_accessed=moved, transcendentals=0),
    )(*args)
    return got[0] if single else got


def shaped(*shape, dtype=bf16):
    return jax.ShapeDtypeStruct(shape, dtype)


def back_perm(perm):
    return [(b, a) for a, b in perm]


def place_kernel(at, ids, gate, tokens, cotangent, own, one, two, three, placer_out, gate_out):
    ids, gate = ids.get(), gate.get()
    y = at[0]
    odd = y % 2
    pair = y // 2
    rows = ids.shape[1]
    e = ids[...]
    expert = lax.broadcasted_iota(jnp.int32, (8, rows), 0)
    onehot = (expert == e).astype(f32)
    before = (
        lax.broadcasted_iota(jnp.int32, (rows, rows), 0)
        < lax.broadcasted_iota(jnp.int32, (rows, rows), 1)
    ).astype(bf16)
    earlier = mm(onehot.astype(bf16), before)
    slot = jnp.sum(onehot * earlier, axis=0, keepdims=True).astype(jnp.int32)
    away = (e - pair + EW) & 3
    near = 1 + 2 * odd
    near = 4 - near
    place = jnp.where(away == 0, 0, jnp.where(away == 2, 3, jnp.where(away == near, 1, 2)))
    target = place * CAP + slot
    placer = (lax.broadcasted_iota(jnp.int32, (rows, rows), 0) == target).astype(f32)
    placed_gate = jnp.sum(placer * gate[...], axis=1, keepdims=True)
    gate_out[...] = jnp.broadcast_to(placed_gate, (rows, rows))
    placer = placer.astype(bf16)
    placer_out[...] = placer
    xs = mm(placer, tokens.get()[...]).astype(bf16)
    ds = (mm(placer, cotangent.get()[...]) * placed_gate).astype(bf16)
    for k, ref in enumerate((own, one, two, three)):
        ref[:, :D] = xs[k * CAP:(k + 1) * CAP]
        ref[:, D:] = ds[k * CAP:(k + 1) * CAP]


def join_kernel(a, b, c, d, out):
    for k, ref in enumerate((a, b, c, d)):
        out[k * CAP:(k + 1) * CAP, :] = ref[...]


def join(parts):
    return call(join_kernel, shaped(4 * CAP, 2 * D), parts, 0, 4 * CAP * 4 * D * 2)


def layer_kernel(n, with_out, touched, *refs):
    blocks, (wg, wu, wd), grads = refs[:n], refs[n:n + 3], refs[n + 3]
    outs = refs[n + 4:]
    row = jnp.zeros((1, HID), f32)
    tile = lax.broadcasted_iota(jnp.int32, (1, HID), 1) // TILE
    for k in range(HID // TILE):
        row = jnp.where(tile == k, touched[0, k].astype(f32), row)
    xs = jnp.concatenate([block[:, :D] for block in blocks], axis=0)
    ds = jnp.concatenate([block[:, D:] for block in blocks], axis=0)
    h = mm(xs, wg[...])
    u = mm(xs, wu[...])
    g = mm(ds, wd[...], NT)
    s = 1.0 / (1.0 + jnp.exp(-h))
    act = (h * s * u).astype(bf16)
    if with_out:
        made = mm(act, wd[...]).astype(bf16)
        for k in range(n):
            outs[k].ref[...] = made[k * 4 * CAP:(k + 1) * 4 * CAP]
            outs[k].send()
    else:
        outs[0][...] = act
    grads[:, :HID] = (g * u * (s * (1.0 + h * (1.0 - s))) * row).astype(bf16)
    grads[:, HID:2 * HID] = (g * (h * s) * row).astype(bf16)
    grads[:, 2 * HID:] = (act.astype(f32) * row).astype(bf16)


def layer(touched, blocks, wg, wu, wd, with_out):
    n = len(blocks)
    rows = n * 4 * CAP
    return call(
        functools.partial(layer_kernel, n, with_out),
        (shaped(rows, 3 * HID),) + ((shaped(4 * CAP, D),) * n if with_out else (shaped(rows, HID),)),
        (touched, *blocks, wg, wu, wd),
        2 * 4 * rows * D * HID, 2 * (3 * D * HID + rows * 3 * D),
        "s" + "v" * (n + 3), "v" + ("h" * n if with_out else "v"),
    )


def near_kernel(touched, a, b, c, d, wg, wu, wd, mine, grads, out):
    join_kernel(a, b, c, d, mine)
    layer_kernel(1, True, touched, mine, wg, wu, wd, grads, out)


def join_layer(touched, parts, wg, wu, wd):
    rows = 4 * CAP
    return call(
        near_kernel,
        (shaped(rows, 2 * D), shaped(rows, 3 * HID), shaped(rows, D)),
        (touched, *parts, wg, wu, wd),
        2 * 4 * rows * D * HID, 2 * (3 * D * HID + rows * 5 * D),
        "s" + "v" * 7, "vvh",
    )


def out_kernel(mine, mates, wd, out_mine, out_mates):
    out_mates.ref[...] = mm(mates[...], wd[...]).astype(bf16)
    out_mates.send()
    out_mine.ref[...] = mm(mine[...], wd[...]).astype(bf16)
    out_mine.send()


STEP = 512


PAIRED = 2


def delta_kernel(xa, xb, xc, xd, ga, gb, gc, gd, *outs):
    grads = jnp.concatenate([ga[...], gb[...], gc[...], gd[...]], axis=0)
    left_over = [PAIRED * SHARE] * len(outs)
    for base, lo, n in ((0, 0, 2), (D, 2 * HID, 1)):
        right = grads[:, lo:lo + n * HID]
        for c0 in range(0, D, STEP):
            cols = slice(base + c0, base + c0 + STEP)
            left = jnp.concatenate([r[:, cols] for r in (xa, xb, xc, xd)], axis=0)
            out = mm(left, right, TN).astype(bf16)
            for k in range(n):
                start = (k if n == 2 else 2) * D + c0
                for rep in range(start // SHARE, (start + STEP - 1) // SHARE + 1):
                    first = max(rep * SHARE, start)
                    last = min((rep + 1) * SHARE, start + STEP)
                    part, off = rep // PAIRED, (rep // PAIRED) * PAIRED * SHARE
                    put = slice(first - off, last - off)
                    outs[part].ref[put, :] = out[first - start:last - start, k * HID:(k + 1) * HID]
                    left_over[part] -= last - first
                    if left_over[part] == 0:
                        outs[part].send()


def delta(xs, grads):
    out = call(
        delta_kernel, shaped(X * Z // PAIRED, PAIRED * SHARE, HID), (*xs, *grads),
        2 * 3 * 16 * CAP * D * HID, 2 * (16 * CAP * 2 * D + 3 * D * HID), "v" * 8, "p", limit=VMEM_WIDE,
    )
    return out.reshape(X, Z, SHARE, HID)


ROWS = 64


def fold_kernel(n, chunks, scale, staged, got, out, total, sems, *rest):
    per = got.shape[1] // chunks
    parts = [pl.ds(c * per, per) for c in range(chunks)]
    stores, loads = [], []
    if staged:
        held, in_sems = rest
        for c, here in enumerate(parts):
            loads.append(pltpu.make_async_copy(got.at[:, here], held.at[:, here], in_sems.at[c]))
            loads[c].start()
        got = held
    for c, here in enumerate(parts):
        if staged:
            loads[c].wait()
        for i in range(c * per, (c + 1) * per):
            value = got[0, i].astype(f32)
            for k in range(1, n):
                value += got[k, i].astype(f32)
            total[i] = (value * scale).astype(bf16)
        stores.append(pltpu.make_async_copy(total.at[here], out.at[here], sems.at[c]))
        stores[c].start()
    for store in stores:
        store.wait()


def fold(got, chunks, scale, staged):
    n = got.shape[0]
    shape = got.shape[1:]
    got = got.reshape(n, -1, ROWS, HID)
    scratch = [pltpu.VMEM(got.shape[1:], bf16), pltpu.SemaphoreType.DMA((chunks,))]
    if staged:
        scratch += [pltpu.VMEM(got.shape, bf16), pltpu.SemaphoreType.DMA((chunks,))]
    out = pl.pallas_call(
        functools.partial(fold_kernel, n, chunks, scale, staged),
        out_shape=shaped(*got.shape[1:]),
        in_specs=[HB if staged else VM],
        out_specs=HB,
        scratch_shapes=scratch,
        compiler_params=pltpu.CompilerParams(vmem_limit_bytes=VMEM_WHOLE if staged else VMEM_WIDE),
        cost_estimate=pl.CostEstimate(flops=0, bytes_accessed=2 * got.size, transcendentals=0),
    )(got)
    return out.reshape(shape)


def add_kernel(a, b, out):
    out.ref[...] = (a[...].astype(f32) + b[...].astype(f32)).astype(bf16)
    out.send()


def add_split_kernel(a, b, c, *outs):
    for k in range(4):
        here = slice(k * CAP, (k + 1) * CAP)
        outs[k].ref[...] = (a[here].astype(f32) + b[here].astype(f32) + c[here].astype(f32)).astype(bf16)
        outs[k].send()


def mixed_kernel(a, b, c, d, gate, placer, out):
    parts = []
    for k, ref in enumerate((a, b, c, d)):
        parts.append((ref[...].astype(f32) * gate[k * CAP:(k + 1) * CAP, :1]).astype(bf16))
    out[...] = mm(placer[...], jnp.concatenate(parts, axis=0), TN).astype(bf16)


def body(tokens, expert_ids, gate_prob, cotangent, w_gate, w_up, w_down, touched):
    rows = tokens.shape[0]
    at = lax.axis_index("y").astype(jnp.int32).reshape(1)
    wg, wu, wd = w_gate[0], w_up[0], w_down[0]
    own, one, two, three, placer, gate = call(
        place_kernel,
        (shaped(CAP, 2 * D),) * 4 + (shaped(rows, rows), shaped(rows, rows, dtype=f32)),
        (at, expert_ids.T, gate_prob[None, :], tokens, cotangent),
        2 * 2 * rows * rows * D, 2 * 4 * rows * D, "shhhh", limit=VMEM_WHOLE,
    )
    near = [own, lax.ppermute(one, "y", PERM1), lax.ppermute(two, "y", PERM2), lax.ppermute(three, "y", PERM3)]
    far = [lax.ppermute(part, "y", PAIR) for part in near]
    mine, ga, p_mine = join_layer(touched, near, wg, wu, wd)
    mates = lax.ppermute(mine, "c", SWAP)
    pair_mine = join(far)
    pair_mates = lax.ppermute(pair_mine, "c", SWAP)
    gb, p_mates = layer(touched, (mates,), wg, wu, wd, True)
    p_got = lax.ppermute(p_mates, "c", SWAP)
    gc, act_mine = layer(touched, (pair_mine,), wg, wu, wd, False)
    gd, act_mates = layer(touched, (pair_mates,), wg, wu, wd, False)

    deltas = delta((mine, mates, pair_mine, pair_mates), (ga, gb, gc, gd))
    over_x = lax.all_to_all(deltas, "x", split_axis=0, concat_axis=0, tiled=True)
    q_mine, q_mates = call(
        out_kernel, (shaped(4 * CAP, D),) * 2, (act_mine, act_mates, wd), 0, 0, "vvv", "hh"
    )
    q_got = lax.ppermute(q_mates, "c", SWAP)
    q_sum = call(add_kernel, shaped(4 * CAP, D), (q_mine, q_got), 0, 0, "vv", "h")
    from_pair = lax.ppermute(q_sum, "y", PAIR)
    blocks = call(
        add_split_kernel, (shaped(CAP, D),) * 4, (p_mine, p_got, from_pair), 0, 0,
        "vvv", "hhhh", limit=VMEM_WIDE,
    )
    back = [blocks[0]] + [
        lax.ppermute(block, "y", back_perm(perm)) for block, perm in zip(blocks[1:], (PERM1, PERM2, PERM3))
    ]
    over_x, back[1:3] = lax.optimization_barrier((over_x, back[1:3]))
    got = lax.all_to_all(fold(over_x, 8, 1.0, True), "z", split_axis=0, concat_axis=0, tiled=True)
    mixed = call(mixed_kernel, shaped(rows, D), (*back, gate, placer), 2 * rows * rows * D, 2 * 2 * rows * D)
    got, mixed = lax.optimization_barrier((got, mixed))
    averaged = fold(got, 3, 1.0 / (X * Z), False).T
    return mixed, averaged


def solution(mesh):
    fine = Mesh(mesh.devices.reshape(X, Z, Y, C), AXES)
    rep, exp = ("x", "z"), ("y", "c")
    return jax.shard_map(
        body,
        mesh=fine,
        in_specs=(
            P(AXES, None),
            P(AXES, None),
            P(AXES),
            P(AXES, None),
            P(rep, None, exp),
            P(rep, None, exp),
            P(rep, exp, None),
            P(rep, exp),
        ),
        out_specs=(P(AXES, None), P(exp, rep)),
        check_vma=False,
    )
```
